768 devices in a mesh: rows: 64 (over y, x, core), grp: 12 (over z).
Axes of the slice: x: 4, y: 8, z: 12, core: 2. Of those that a mesh axis runs over, the one named last changes fastest.
Arguments:
- points: float32 [196608, 440], P(('rows', 'grp')), may hold values from -5 to 5
- targets: float32 [196608, 147], P(('rows', 'grp')), may hold values from -6 to 6
- coefs_start: float32 [196608, 147], P(('rows', 'grp')), may hold values from -0.6 to 0.6
- block_index: int32 [3, 256], replicated, may hold values from 0 to 196607, as said below
Outputs:
- coefficients: float32 [196608, 147], P(('rows', 'grp'))
The draws below stay inside these ranges and needn't reach their ends.
Inputs may be any that keep to these rules, and one draw needn't show every extreme that they name: `block_index`: devices of the rows+grp axis are numbered r * 12 + g, and device d holds rows d * 256 to (d + 1) * 256 - 1. For each block, entries r * 4 to (r + 1) * 4 - 1 are distinct rows held by device (r, g) for one grp index g of that block, the same g for all r. Different blocks may share rows. Block 0 holds row 0 and block 1 holds row 196607.
All inputs are finite; a program needn't handle non-finite values.
Results may differ from the reference program's by a relative error of at most 0.0003.
Values sent between devices are 32-bit elements; how exact they have to be, the bound alone decides.
A program may use at most 32 MiB of HBM per device.

```python
import jax
import jax.numpy as jnp
from jax import lax

FEATURES = 440
CLASSES = 147
ROWS_DEV = 256
BLOCK = 256
BLOCKS = 3
BLOCK_PART = 4
POINTS = 196608
N_ROWS = 64
N_GRP = 12


def block_plan(key):
    folded = jax.random.fold_in(key, 11)
    first_key, second_key = jax.random.split(folded)
    holders = jax.random.randint(first_key, (BLOCKS,), 0, N_GRP).astype(jnp.int32)
    holders = holders.at[0].set(0).at[1].set(N_GRP - 1)
    many_keys = jax.random.split(second_key, BLOCKS * N_ROWS)
    perms = jax.vmap(lambda single: jax.random.permutation(single, ROWS_DEV))(many_keys)
    perms = perms.reshape(BLOCKS, N_ROWS, ROWS_DEV).astype(jnp.int32)
    leading = perms[:, :, 0]
    leading = leading.at[0, 0].set(0).at[1, N_ROWS - 1].set(ROWS_DEV - 1)
    rotated = (perms - perms[:, :, :1] + leading[:, :, None]) % ROWS_DEV
    offsets = rotated[:, :, :BLOCK_PART]
    device_no = jnp.arange(N_ROWS, dtype=jnp.int32)[None, :, None] * N_GRP + holders[:, None, None]
    return (device_no * ROWS_DEV + offsets).reshape(BLOCKS, BLOCK).astype(jnp.int32)


def draw_block_index(key, part):
    return block_plan(key)


def draw_points(key, part):
    folded = jax.random.fold_in(key, 23)
    latent_key, factor_key, jitter_key = jax.random.split(folded, 3)
    latent = jax.random.uniform(latent_key, (POINTS, 8), jnp.float32, -2.8, 2.8)
    factors = jax.random.uniform(factor_key, (FEATURES,), jnp.float32, 0.75, 1.25)
    jitter = jnp.clip(0.3 * jax.random.normal(jitter_key, (POINTS, FEATURES), jnp.float32), -1.2, 1.2)
    columns = jnp.arange(FEATURES, dtype=jnp.int32) % 8
    return (latent[:, columns] * factors[None, :] + jitter).astype(jnp.float32)


def levels(rng, dims, shards, low, largest):
    def one(axis_at, shards_of):
        steps = jax.random.uniform(jax.random.fold_in(jax.random.fold_in(rng, 6), axis_at), (shards_of,), jnp.float32, low / len(shards), largest / len(shards))
        return jnp.repeat(jnp.exp(steps), dims[axis_at] // shards_of).reshape((-1,) + (1,) * (len(dims) - axis_at - 1))

    gain = one(*shards[0])
    for cut in shards[1:]:
        gain = gain * one(*cut)
    return gain


def gaussian(stream_key, dims, spread, limit, cuts=(), held_as=jnp.bfloat16):
    array = jax.random.normal(stream_key, dims, jnp.float32) * spread
    if len(cuts) > 0:
        array = levels(stream_key, dims, cuts, -0.22, 0.18) * array
    return jnp.clip(array, min=-limit, max=limit).astype(held_as)


def setup_inputs(seed: int = 0) -> dict:
    keys = jax.random.split(jax.random.key(seed), 5)
    points = draw_points(jax.random.fold_in(keys[4], 71), 0)
    targets = gaussian(keys[1], (POINTS, CLASSES), 1.0, 6.0, ((0, 768),), jnp.float32)
    coefs_start = gaussian(keys[2], (POINTS, CLASSES), 0.1, 0.6, ((0, 768),), jnp.float32)
    block_index = draw_block_index(jax.random.fold_in(keys[4], 71), 0)
    return dict(points=points, targets=targets, coefs_start=coefs_start, block_index=block_index)


ridge = 0.5

def kernel(left, right):
    left_sq = jnp.sum(left * left, axis=1)
    right_sq = jnp.sum(right * right, axis=1)
    cross = jnp.dot(left.astype(jnp.float32), right.T.astype(jnp.float32), precision=lax.Precision.HIGHEST, preferred_element_type=jnp.float32)
    dist = left_sq[:, None] + right_sq[None, :] - 2.0 * cross
    return jnp.exp(-2.0 * dist / FEATURES)

def reference(points, targets, coefs_start, block_index):
    coefficients = coefs_start
    for current in range(BLOCKS):
        rows_now = block_index[current]
        block_points = points[rows_now]
        slabs = points.reshape(-1, ROWS_DEV, FEATURES)
        coef_slabs = coefficients.reshape(-1, ROWS_DEV, CLASSES)

        def accumulate(carry, pair):
            return (carry + jnp.dot(kernel(block_points, pair[0]).astype(jnp.float32), pair[1].astype(jnp.float32), precision=lax.Precision.HIGHEST, preferred_element_type=jnp.float32), None)
        summed, unused = lax.scan(accumulate, jnp.zeros((BLOCK, CLASSES), jnp.float32), (slabs, coef_slabs))
        system = kernel(block_points, block_points) + ridge * jnp.eye(BLOCK, dtype=jnp.float32)
        right_side = targets[rows_now] - ridge * coefficients[rows_now] - summed
        factor = jnp.linalg.cholesky(system)
        change = jax.scipy.linalg.cho_solve((factor, True), right_side)
        coefficients = coefficients.at[rows_now].add(change)
    return coefficients
```

```python
import functools

import jax
import jax.numpy as jnp
from jax import lax
from jax.experimental import pallas as pl
from jax.experimental.pallas import tpu as pltpu
from jax.sharding import PartitionSpec as P

HIGH = lax.Precision.HIGHEST
VMEM = pl.BlockSpec(memory_space=pltpu.VMEM)
SMEM = pl.BlockSpec(memory_space=pltpu.SMEM)
MESH = pl.DeviceIdType.MESH
NY, NX, NC, NZ = 8, 4, 2, 12
PART = 4
CHUNKS = 4
PAD = 512
ridge = 0.5


def dot(a, b, ca=1, cb=0):
    return lax.dot_general(a, b, (((ca,), (cb,)), ((), ())), precision=HIGH, preferred_element_type=jnp.float32)


def row_of(v, k):
    return jnp.broadcast_to(v[k:k + 1, :], v.shape)


def lane_of(v, k):
    return jnp.broadcast_to(v[:, k:k + 1], v.shape)


def eliminate(rows, t):
    place = lax.broadcasted_iota(jnp.int32, (8, 128), 0)
    top = rows[0]
    spread = [[lane_of(v, j) for j in range(8)] for v in rows[1:]]
    cols = [lane_of(top, j) for j in range(8)]
    forward = top
    full = top
    scale = jnp.zeros((8, 128), jnp.float32)
    for k in range(8):
        pivot = row_of(cols[k], k)
        inverse = 1.0 / pivot
        scale = jnp.where(place == k, inverse, scale)
        step = cols[k] * inverse
        both = jnp.where(place == k, 0.0, step)
        below = jnp.where(place > k, step, 0.0)
        for j in range(k + 1, 8):
            cols[j] = cols[j] - both * row_of(cols[j], k)
        forward = forward - below * row_of(forward, k)
        full = full - both * row_of(full, k)
    solved = full * scale
    done = forward * jnp.sqrt(scale)
    lines = [row_of(solved, j) for j in range(8)]
    out = []
    for p in range(1, 8):
        s = spread[p - 1]
        terms = [s[j] * lines[j] for j in range(8)]
        total = ((terms[0] + terms[1]) + (terms[2] + terms[3])) + ((terms[4] + terms[5]) + (terms[6] + terms[7]))
        live = jnp.where(t + p < 8, 1.0, 0.0).astype(jnp.float32)
        out.append(rows[p] - live * total)
    out.append(done)
    return [pltpu.roll(v, 120, 1) for v in out]


def factor64(blocks):
    n = len(blocks)
    unit = (lax.broadcasted_iota(jnp.int32, (64, 64), 0) == lax.broadcasted_iota(jnp.int32, (64, 64), 1)).astype(jnp.float32)
    state = []
    for b in blocks:
        w = jnp.concatenate([b, unit], axis=1)
        state += [w[8 * p:8 * p + 8, :] for p in range(8)]
    def group(t, state):
        out = []
        for m in range(n):
            out += eliminate(list(state[8 * m:8 * m + 8]), t)
        return tuple(out)
    state = lax.fori_loop(0, 8, group, tuple(state))
    return [jnp.concatenate(state[8 * m:8 * m + 8], axis=0)[:, :64] for m in range(n)]


def factor256(work):
    n = work.shape[0]
    for j in range(4):
        lo, hi = 64 * j, 64 * j + 64
        invs = factor64([work[m, lo:hi, lo:hi] for m in range(n)])
        for m in range(n):
            rows = dot(invs[m], work[m, lo:hi, :])
            work[m, lo:hi, :] = rows
            if j < 3:
                work[m, hi:, :] = work[m, hi:, :] - dot(rows[:, hi:256], rows, 0, 0)


def iota(shape, axis):
    return lax.broadcasted_iota(jnp.int32, shape, axis)


def spot():
    line = lax.axis_index("rows")
    return line // (NX * NC), line // NC % NX, line % NC, lax.axis_index("grp")


def device(y, x, c, z):
    return ((y * NX + x) * NC + c, z)


def partner(axis, step):
    y, x, c, z = spot()
    if axis == "y":
        return device((y + step) % NY, x, c, z)
    if axis == "x":
        return device(y, (x + step) % NX, c, z)
    if axis == "z":
        return device(y, x, c, (z + step) % NZ)
    return device(y, x, (c + step) % NC, z)


SIZES = {"y": NY, "x": NX, "z": NZ, "c": NC}


def greet():
    barrier = pltpu.get_barrier_semaphore()
    count = 0
    for axis, size in SIZES.items():
        for step in range(1, size):
            pl.semaphore_signal(barrier, inc=1, device_id=partner(axis, step), device_id_type=MESH)
            count += 1
    pl.semaphore_wait(barrier, count)


class Mail:
    def __init__(self, send_sem, recv_sem):
        self.send_sem, self.recv_sem, self.used, self.sent = send_sem, recv_sem, 0, []

    def send(self, axis, step, source, target):
        copy = pltpu.make_async_remote_copy(
            src_ref=source,
            dst_ref=target,
            send_sem=self.send_sem.at[self.used],
            recv_sem=self.recv_sem.at[self.used],
            device_id=partner(axis, step),
            device_id_type=MESH,
        )
        copy.start()
        self.used += 1
        self.sent.append(copy)
        return copy

    def spread(self, axis, source, target):
        return [self.send(axis, step, source, target) for step in range(1, SIZES[axis])]

    def close(self):
        for copy in self.sent:
            copy.wait_send()


def arrive(copies):
    for copy in copies:
        copy.wait_recv()


COPIES_GATHER = 2 * (NZ - 1) + (NX - 1) + (NY - 1) + (NX - 1) + (NY - 1) + (NX - 1) + (NY - 1) + (NZ - 1) + 1


def gather_body(points_ref, index_ref, out_ref, picked, landed, send_sem, recv_sem):
    y, x, c, z = spot()
    me = lax.axis_index("rows") * NZ + z
    line = lax.axis_index("rows")
    count, width = points_ref.shape
    mail = Mail(send_sem, recv_sem)
    blocks = index_ref.shape[0]
    picked[...] = jnp.zeros_like(picked)
    for k in range(blocks):
        for i in range(PART):
            row = index_ref[k, line * PART + i]
            mine = row // count == me
            value = points_ref[pl.ds(row % count, 1), :]
            value = jnp.where(mine, value, 0.0)
            for ch in range(CHUNKS):
                lo, hi = 128 * ch, min(128 * ch + 128, width)
                picked[PART * k + i, ch : ch + 1, : hi - lo] = value[:, lo:hi]
    greet()
    k, i = z // PART, z % PART
    step1 = [mail.send("z", s, picked.at[(z + s) % NZ], landed.at[s]) for s in range(1, NZ)]
    arrive(step1)
    row = picked[z]
    for s in range(1, NZ):
        row = row + landed[s]
    for ch in range(CHUNKS):
        out_ref[c, ch, x, k, y, pl.ds(i, 1), :] = row[ch : ch + 1, :]
    one = out_ref.at[c, 0:3, x, k, y, pl.ds(i, 1)]
    ab1 = mail.spread("z", one, one)
    one = out_ref.at[c, 3, x, k, y, pl.ds(i, 1)]
    c1 = mail.spread("x", one, one)
    arrive(c1)
    some = out_ref.at[c, 3, :, k, y, pl.ds(i, 1)]
    c2 = mail.spread("y", some, some)
    arrive(ab1)
    some = out_ref.at[c, 0:2, x, :, y]
    a2 = mail.spread("y", some, some)
    some = out_ref.at[c, 2, x, :, y]
    b2 = mail.spread("x", some, some)
    arrive(c2)
    many = out_ref.at[c, 3, :, k, :, pl.ds(i, 1)]
    c3 = mail.spread("z", many, many)
    arrive(b2)
    many = out_ref.at[c, 2, :, :, y]
    b3 = mail.spread("y", many, many)
    arrive(a2)
    many = out_ref.at[c, 0:2, x]
    a3 = mail.spread("x", many, many)
    arrive(a3)
    arrive(b3)
    arrive(c3)
    last = [mail.send("c", 1, out_ref.at[c], out_ref.at[c])]
    arrive(last)
    mail.close()


def squares(rows):
    return dot(jnp.ones((8, rows.shape[1]), jnp.float32), rows * rows, 1, 1)[:1]


def kernel_block(left, right, width):
    cross = sum(dot(a, b, 1, 1) for a, b in zip(left, right))
    left_sq = sum(jnp.sum(a * a, axis=1, keepdims=True) for a in left)
    right_sq = sum(squares(b) for b in right)
    return jnp.exp((left_sq + right_sq - 2.0 * cross) * (-2.0 / width))


def block_chunks(block_ref, k):
    return [jnp.concatenate([block_ref[c, ch, :, k].reshape(-1, 128) for c in range(NC)]) for ch in range(CHUNKS)]


def partial_body(block_ref, points_ref, targets_ref, coefs_ref, index_ref, out_ref, work):
    me = lax.axis_index("rows") * NZ + lax.axis_index("grp")
    coefs = coefs_ref[...]
    count, width = points_ref.shape
    classes = coefs.shape[1]
    start = targets_ref[...] - ridge * coefs
    work[...] = jnp.zeros_like(work)
    work[:, :width] = points_ref[...]
    points = [work[:, 128 * ch : 128 * ch + 128] for ch in range(CHUNKS)]
    out_ref[...] = jnp.zeros_like(out_ref)
    for k in range(block_ref.shape[3]):
        kern = kernel_block(points, block_chunks(block_ref, k), width)
        here = index_ref[k : k + 1, :] == iota(kern.shape, 0) + me * count
        total = dot(coefs, kern, 0, 0) - dot(start, here.astype(jnp.float32), 0, 0)
        for c in range(NC):
            out_ref[c, 152 * k : 152 * k + classes, :] = total[:, 128 * c : 128 * c + 128]


def solve_body(block_ref, index_ref, out_ref, work):
    line = lax.axis_index("rows")
    width = 440
    n, size = work.shape[0], work.shape[1]
    unit = (iota((size, size), 0) == iota((size, size), 1)).astype(jnp.float32)
    parts = [block_chunks(block_ref, k) for k in range(n)]
    rows = [index_ref[k : k + 1, :].astype(jnp.float32) for k in range(n)]
    for k in range(n):
        work[k, :, :size] = kernel_block(parts[k], parts[k], width) + ridge * unit
        work[k, :, size:] = unit
    factor256(work)
    link = {}
    for k in range(1, n):
        column = jnp.sum(jnp.where(unit > 0.0, rows[k], 0.0), axis=1, keepdims=True)
        for j in range(k):
            same = (column == rows[j]).astype(jnp.float32)
            link[k, j] = kernel_block(parts[k], parts[j], width) + ridge * same
    y, x, c, z = spot()
    height = out_ref.shape[0]
    pick, lane = iota((height, size), 0), iota((height, size), 1)
    found = {}
    for k in reversed(range(n)):
        mine = (pick // PART == k) & (lane == ((c * NX + x) * NY + y) * PART + pick % PART)
        value = mine.astype(jnp.float32)
        for j in range(k + 1, n):
            value = value - dot(found[j], link[j, k])
        inverse = work[k, :, size:]
        found[k] = dot(dot(value, inverse, 1, 1), inverse)
        out_ref[:, size * k : size * (k + 1)] = found[k]


COPIES_TOTAL = 1 + (NX - 1) + (NY - 1) + (NZ - 1) + (NY - 1) + (NX - 1) + 1


def total_body(part_ref, out_ref, from_c, from_x, from_y, from_z, sum_c, sum_x, sum_y, send_sem, recv_sem):
    y, x, c, z = spot()
    mail = Mail(send_sem, recv_sem)
    tall, low = PAD // NX, PAD // NX // NY
    greet()
    arrive([mail.send("c", 1, part_ref.at[1 - c], from_c)])
    sum_c[...] = part_ref[c] + from_c[...]
    copies = []
    for s in range(1, NX):
        piece = sum_c.at[pl.ds(pl.multiple_of((x + s) % NX * tall, tall), tall)]
        copies.append(mail.send("x", s, piece, from_x.at[s]))
    arrive(copies)
    total = sum_c[pl.ds(pl.multiple_of(x * tall, tall), tall)]
    for s in range(1, NX):
        total = total + from_x[s]
    sum_x[...] = total
    copies = []
    for s in range(1, NY):
        piece = sum_x.at[pl.ds(pl.multiple_of((y + s) % NY * low, low), low)]
        copies.append(mail.send("y", s, piece, from_y.at[s]))
    arrive(copies)
    total = sum_x[pl.ds(pl.multiple_of(y * low, low), low)]
    for s in range(1, NY):
        total = total + from_y[s]
    sum_y[...] = total
    arrive([mail.send("z", s, sum_y, from_z.at[s]) for s in range(1, NZ)])
    for s in range(1, NZ):
        total = total + from_z[s]
    mine = pl.ds(pl.multiple_of(x * tall + y * low, low), low)
    out_ref[c, mine, :] = total
    arrive(mail.spread("y", out_ref.at[c, mine], out_ref.at[c, mine]))
    mine = pl.ds(pl.multiple_of(x * tall, tall), tall)
    arrive(mail.spread("x", out_ref.at[c, mine], out_ref.at[c, mine]))
    arrive([mail.send("c", 1, out_ref.at[c], out_ref.at[c])])
    mail.close()


def place_body(total_ref, rows_ref, coefs_ref, index_ref, out_ref, change_ref):
    line = lax.axis_index("rows")
    me = line * NZ + lax.axis_index("grp")
    count, classes = coefs_ref.shape
    change = jnp.zeros(change_ref.shape, jnp.float32)
    for k in range(index_ref.shape[0]):
        for c in range(NC):
            at = 256 * k + 128 * c
            change = change - dot(rows_ref[:, at : at + 128], total_ref[c, 152 * k : 152 * k + classes, :], 1, 1)
    change_ref[...] = change
    out_ref[...] = coefs_ref[...]
    for k in range(index_ref.shape[0]):
        for i in range(PART):
            row = index_ref[k, line * PART + i]
            mine = jnp.where(row // count == me, 1.0, 0.0).astype(jnp.float32)
            at = pl.ds(row % count, 1)
            out_ref[at, :] = out_ref[at, :] + mine * change_ref[pl.ds(PART * k + i, 1), :]


def body(points, targets, coefs, block_index):
    blocks, size = block_index.shape
    count, width = points.shape
    classes = targets.shape[1]
    order = block_index.reshape(blocks, NY, NX, NC, PART).transpose(0, 3, 2, 1, 4).reshape(blocks, size)
    params = pltpu.CompilerParams(vmem_limit_bytes=40 << 20)
    f32 = jnp.float32
    arrived = pl.pallas_call(
        gather_body,
        out_shape=jax.ShapeDtypeStruct((NC, CHUNKS, NX, blocks, NY, PART, 128), f32),
        in_specs=[VMEM, SMEM],
        out_specs=VMEM,
        scratch_shapes=[
            pltpu.VMEM((NZ, CHUNKS, 128), f32),
            pltpu.VMEM((NZ, CHUNKS, 128), f32),
            pltpu.SemaphoreType.DMA((COPIES_GATHER,)),
            pltpu.SemaphoreType.DMA((COPIES_GATHER,)),
        ],
        compiler_params=pltpu.CompilerParams(vmem_limit_bytes=40 << 20, collective_id=1, has_side_effects=True),
        name="gather_blocks",
    )(points, block_index)
    arrived = arrived.reshape(NC, CHUNKS, NX, blocks, NY * PART, 128)
    partial_value = pl.pallas_call(
        partial_body,
        out_shape=jax.ShapeDtypeStruct((NC, PAD, 128), f32),
        in_specs=[VMEM] * 5,
        out_specs=VMEM,
        scratch_shapes=[pltpu.VMEM((count, 128 * CHUNKS), f32)],
        compiler_params=params,
        name="partial_sums",
    )(arrived, points, targets, coefs, order)
    total = pl.pallas_call(
        total_body,
        out_shape=jax.ShapeDtypeStruct((NC, PAD, 128), f32),
        in_specs=[VMEM],
        out_specs=VMEM,
        scratch_shapes=[
            pltpu.VMEM((PAD, 128), f32),
            pltpu.VMEM((NX, PAD // NX, 128), f32),
            pltpu.VMEM((NY, PAD // NX // NY, 128), f32),
            pltpu.VMEM((NZ, PAD // NX // NY, 128), f32),
            pltpu.VMEM((PAD, 128), f32),
            pltpu.VMEM((PAD // NX, 128), f32),
            pltpu.VMEM((PAD // NX // NY, 128), f32),
            pltpu.SemaphoreType.DMA((COPIES_TOTAL,)),
            pltpu.SemaphoreType.DMA((COPIES_TOTAL,)),
        ],
        compiler_params=pltpu.CompilerParams(vmem_limit_bytes=40 << 20, collective_id=2, has_side_effects=True),
        name="total_sums",
    )(partial_value)
    rows = pl.pallas_call(
        solve_body,
        out_shape=jax.ShapeDtypeStruct((16, blocks * size), f32),
        in_specs=[VMEM] * 2,
        out_specs=VMEM,
        scratch_shapes=[pltpu.VMEM((blocks, size, 2 * size), f32)],
        compiler_params=params,
        name="solve_rows",
    )(arrived, order)
    return pl.pallas_call(
        place_body,
        out_shape=jax.ShapeDtypeStruct(coefs.shape, f32),
        in_specs=[VMEM, VMEM, VMEM, SMEM],
        out_specs=VMEM,
        scratch_shapes=[pltpu.VMEM((16, classes), f32)],
        compiler_params=params,
        name="place_change",
    )(total, rows, coefs, block_index)


def solution(mesh):
    return jax.shard_map(
        body,
        mesh=mesh,
        in_specs=(
            P(("rows", "grp"), None),
            P(("rows", "grp"), None),
            P(("rows", "grp"), None),
            P(),
        ),
        out_specs=P(("rows", "grp"), None),
        check_vma=False,
    )
```

```python
import functools

import jax
import jax.numpy as jnp
from jax import lax
from jax.experimental import pallas as pl
from jax.experimental.pallas import tpu as pltpu
from jax.sharding import PartitionSpec as P

HIGH = lax.Precision.HIGHEST
VMEM = pl.BlockSpec(memory_space=pltpu.VMEM)
SMEM = pl.BlockSpec(memory_space=pltpu.SMEM)
ANY = pl.BlockSpec(memory_space=pl.ANY)
MESH = pl.DeviceIdType.MESH
NY, NX, NC, NZ = 8, 4, 2, 12
PART = 4
CHUNKS = 4
PAD = 512
TALL, LOW = PAD // NX, PAD // NX // NY
CLASS_ROWS = 152
ROLES = 3
ridge = 0.5


def dot(a, b, ca=1, cb=0):
    return lax.dot_general(a, b, (((ca,), (cb,)), ((), ())), precision=HIGH, preferred_element_type=jnp.float32)


def row_of(v, k):
    return jnp.broadcast_to(v[k:k + 1, :], v.shape)


def lane_of(v, k):
    return jnp.broadcast_to(v[:, k:k + 1], v.shape)


def eliminate(rows, t):
    place = lax.broadcasted_iota(jnp.int32, (8, 128), 0)
    top = rows[0]
    spread = [[lane_of(v, j) for j in range(8)] for v in rows[1:]]
    cols = [lane_of(top, j) for j in range(8)]
    forward = top
    full = top
    scale = jnp.zeros((8, 128), jnp.float32)
    for k in range(8):
        pivot = row_of(cols[k], k)
        inverse = 1.0 / pivot
        scale = jnp.where(place == k, inverse, scale)
        step = cols[k] * inverse
        both = jnp.where(place == k, 0.0, step)
        below = jnp.where(place > k, step, 0.0)
        for j in range(k + 1, 8):
            cols[j] = cols[j] - both * row_of(cols[j], k)
        forward = forward - below * row_of(forward, k)
        full = full - both * row_of(full, k)
    solved = full * scale
    done = forward * jnp.sqrt(scale)
    lines = [row_of(solved, j) for j in range(8)]
    out = []
    for p in range(1, 8):
        s = spread[p - 1]
        terms = [s[j] * lines[j] for j in range(8)]
        total = ((terms[0] + terms[1]) + (terms[2] + terms[3])) + ((terms[4] + terms[5]) + (terms[6] + terms[7]))
        live = jnp.where(t + p < 8, 1.0, 0.0).astype(jnp.float32)
        out.append(rows[p] - live * total)
    out.append(done)
    return [pltpu.roll(v, 120, 1) for v in out]


def factor64(blocks):
    n = len(blocks)
    unit = (lax.broadcasted_iota(jnp.int32, (64, 64), 0) == lax.broadcasted_iota(jnp.int32, (64, 64), 1)).astype(jnp.float32)
    state = []
    for b in blocks:
        w = jnp.concatenate([b, unit], axis=1)
        state += [w[8 * p:8 * p + 8, :] for p in range(8)]
    def group(t, state):
        out = []
        for m in range(n):
            out += eliminate(list(state[8 * m:8 * m + 8]), t)
        return tuple(out)
    state = lax.fori_loop(0, 8, group, tuple(state))
    return [jnp.concatenate(state[8 * m:8 * m + 8], axis=0)[:, :64] for m in range(n)]


def iota(shape, axis):
    return lax.broadcasted_iota(jnp.int32, shape, axis)


def spot():
    line = lax.axis_index("rows")
    return line // (NX * NC), line // NC % NX, line % NC, lax.axis_index("grp")


def device(y, x, c, z):
    return ((y * NX + x) * NC + c, z)


def partner(axis, step):
    y, x, c, z = spot()
    if axis == "y":
        return device((y + step) % NY, x, c, z)
    if axis == "x":
        return device(y, (x + step) % NX, c, z)
    if axis == "z":
        return device(y, x, c, (z + step) % NZ)
    return device(y, x, (c + step) % NC, z)


SIZES = {"y": NY, "x": NX, "z": NZ, "c": NC}


def greet():
    barrier = pltpu.get_barrier_semaphore()
    count = 0
    for axis, size in SIZES.items():
        for step in range(1, size):
            pl.semaphore_signal(barrier, inc=1, device_id=partner(axis, step), device_id_type=MESH)
            count += 1
    return count


class Mail:
    def __init__(self, send_sem, recv_sem):
        self.send_sem, self.recv_sem, self.used, self.sent = send_sem, recv_sem, 0, []

    def send(self, axis, step, source, target):
        copy = pltpu.make_async_remote_copy(
            src_ref=source,
            dst_ref=target,
            send_sem=self.send_sem.at[self.used],
            recv_sem=self.recv_sem.at[self.used],
            device_id=partner(axis, step),
            device_id_type=MESH,
        )
        copy.start()
        self.used += 1
        self.sent.append(copy)
        return copy

    def spread(self, axis, source, target):
        return [self.send(axis, step, source, target) for step in range(1, SIZES[axis])]

    def close(self):
        for copy in self.sent:
            copy.wait_send()


def arrive(copies):
    for copy in copies:
        copy.wait_recv()


COPIES = (
    1 + 1 + 2 * (NZ - 1) + (NX - 1) + (NY - 1) + (NX - 1) + (NY - 1) + (NX - 1) + (NY - 1) + (NZ - 1) + 1
    + (NX - 1) + (NY - 1) + (NZ - 1) + (NY - 1) + (NX - 1) + 1
)


def half_rows(blocks_ref, c, k):
    return jnp.concatenate([blocks_ref[c, ch, :, k].reshape(-1, 128) for ch in range(CHUNKS)], axis=1)


def whole_rows(blocks_ref, k):
    return jnp.concatenate([half_rows(blocks_ref, c, k) for c in range(NC)], axis=0)


def kernel_block(left, right, width):
    cross = dot(left, right, 1, 1)
    left_sq = jnp.sum(left * left, axis=1, keepdims=True)
    right_sq = dot(jnp.ones((8, right.shape[1]), jnp.float32), right * right, 1, 1)[:1]
    return jnp.exp((left_sq + right_sq - 2.0 * cross) * (-2.0 / width))


def kernel_points(left, points, width):
    cross = dot(left, points, 1, 0)
    left_sq = jnp.sum(left * left, axis=1, keepdims=True)
    right_sq = jnp.sum(points * points, axis=0, keepdims=True)
    return jnp.exp((left_sq + right_sq - 2.0 * cross) * (-2.0 / width))


def identity(size):
    return (iota((size, size), 0) == iota((size, size), 1)).astype(jnp.float32)


def factor_step(work, j):
    lo, hi = 64 * j, 64 * j + 64
    inverse = factor64([work[lo:hi, lo:hi]])[0]
    rows = dot(inverse, work[lo:hi, :])
    work[lo:hi, :] = rows
    if j < 3:
        work[hi:, :] = work[hi:, :] - dot(rows[:, hi:256], rows, 0, 0)


def whole_body(
    pt_hbm, tt_hbm, ct_hbm, index_ref, index_hbm, out_ref,
    points, points2, targets, coefs, coefs2, index_rows, picked, landed, blocks,
    sums, from_x, from_y, from_z, sum_x, sum_y, total,
    work, link, hand, thin_in, solved,
    local_sem, send_sem, recv_sem, role_send, role_recv,
):
    y, x, c, z = spot()
    line = lax.axis_index("rows")
    me = line * NZ + z
    width, count = pt_hbm.shape
    classes = ct_hbm.shape[0]
    nblocks = index_ref.shape[0]
    mail = Mail(send_sem, recv_sem)

    greeted = greet()
    loads = [
        pltpu.make_async_copy(pt_hbm, points.at[pl.ds(0, width)], local_sem.at[0]),
        pltpu.make_async_copy(tt_hbm, targets, local_sem.at[1]),
        pltpu.make_async_copy(ct_hbm, coefs, local_sem.at[2]),
        pltpu.make_async_copy(index_hbm, index_rows, local_sem.at[3]),
    ]
    for load in loads:
        load.start()
    points[width:, :] = jnp.zeros((points.shape[0] - width, count), jnp.float32)
    points2[width:, :] = jnp.zeros((points.shape[0] - width, count), jnp.float32)
    row_no = iota((16, count), 0)
    mine = jnp.full((16, count), -1, jnp.int32)
    for k in range(nblocks):
        for i in range(PART):
            mine = jnp.where(row_no == PART * k + i, index_ref[k, line * PART + i], mine)
    owned = (mine == iota((16, count), 1) + me * count).astype(jnp.float32)
    for load in loads:
        load.wait()
    rows = dot(owned, points[...], 1, 1)
    for ch in range(CHUNKS):
        picked[ch] = rows[:, 128 * ch : 128 * ch + 128]
    start = dot(targets[...] - ridge * coefs[...], owned, 1, 1)
    sums[...] = jnp.zeros_like(sums)
    pick, lane = iota((16, 128), 0), iota((16, 128), 1)
    for k in range(nblocks):
        at = (pick // PART == k) & (lane == x * 32 + pick % PART * 8 + y)
        sums[CLASS_ROWS * k : CLASS_ROWS * k + classes, :] = -dot(start, at.astype(jnp.float32))
    pl.semaphore_wait(pltpu.get_barrier_semaphore(), greeted)

    k, i = z // PART, z % PART
    my_y = pl.ds(y, 1)
    step1 = [mail.send("z", s, picked.at[:, pl.ds((z + s) % NZ, 1)], landed.at[s]) for s in range(1, NZ)]
    pair = [mail.send("c", 1, points.at[pl.ds(0, width)], points2.at[pl.ds(0, width)])]
    pair.append(mail.send("c", 1, coefs, coefs2))
    arrive(step1)
    row = picked[:, pl.ds(z, 1), :]
    for s in range(1, NZ):
        row = row + landed[s]
    for ch in range(CHUNKS):
        blocks[c, ch, x, k, i, my_y, :] = row[ch]
    one = blocks.at[c, 0:3, x, k, i, my_y]
    ab1 = mail.spread("z", one, one)
    one = blocks.at[c, 3, x, k, i, my_y]
    c1 = mail.spread("x", one, one)
    arrive(c1)
    some = blocks.at[c, 3, :, k, i, my_y]
    c2 = mail.spread("y", some, some)
    arrive(ab1)
    some = blocks.at[c, 0:2, x, :, :, my_y]
    a2 = mail.spread("y", some, some)
    some = blocks.at[c, 2, x, :, :, my_y]
    b2 = mail.spread("x", some, some)
    arrive(c2)
    many = blocks.at[c, 3, :, k, i]
    c3 = mail.spread("z", many, many)
    arrive(b2)
    many = blocks.at[c, 2, :, :, :, my_y]
    b3 = mail.spread("y", many, many)
    arrive(a2)
    many = blocks.at[c, 0:2, x]
    a3 = mail.spread("x", many, many)
    arrive(pair)
    arrive(a3)
    arrive(b3)
    arrive(c3)
    other = [mail.send("c", 1, blocks.at[c], blocks.at[c])]

    half = jnp.concatenate([half_rows(blocks, c, k) for k in range(nblocks)], axis=0)
    term = dot(coefs[...], kernel_points(half, points[...], width), 1, 1)
    term = term + dot(coefs2[...], kernel_points(half, points2[...], width), 1, 1)
    for k in range(nblocks):
        at = slice(CLASS_ROWS * k, CLASS_ROWS * k + classes)
        sums[at, :] = sums[at, :] + term[:, 128 * k : 128 * k + 128]

    def tall_at(x):
        return pl.ds(pl.multiple_of(x * TALL, TALL), TALL)

    def low_at(y):
        return pl.ds(pl.multiple_of(y * LOW, LOW), LOW)

    sent = [mail.send("x", s, sums.at[tall_at((x + s) % NX)], from_x.at[s]) for s in range(1, NX)]
    role = z % ROLES
    arrive(other)
    own = whole_rows(blocks, role)
    work[:, 256:] = identity(256)
    work[:, :256] = kernel_block(own, own, width) + ridge * identity(256)
    factor_step(work, 0)
    arrive(sent)
    value = sums[tall_at(x)]
    for s in range(1, NX):
        value = value + from_x[s]
    sum_x[...] = value
    sent = [mail.send("y", s, sum_x.at[low_at((y + s) % NY)], from_y.at[s]) for s in range(1, NY)]
    factor_step(work, 1)
    arrive(sent)
    value = sum_x[low_at(y)]
    for s in range(1, NY):
        value = value + from_y[s]
    sum_y[...] = value
    sent = [mail.send("z", s, sum_y, from_z.at[s]) for s in range(1, NZ)]

    lane = iota((256, 256), 1)
    at = iota((256, 256), 0)
    line_of = (lane % 8 * NX + lane // 32 % 4) * NC + lane // 128
    order = (at == line_of * PART + lane // 8 % 4).astype(jnp.float32)
    numbers = dot(index_rows[...].astype(jnp.float32), order)

    def link_of(k, j):
        column = jnp.sum(jnp.where(at == lane, numbers[k : k + 1, :], 0.0), axis=1, keepdims=True)
        same = (column == numbers[j : j + 1, :]).astype(jnp.float32)
        return kernel_block(whole_rows(blocks, k), whole_rows(blocks, j), width) + ridge * same

    @pl.when(role == 2)
    def _():
        link[0] = link_of(2, 0)
        link[1] = link_of(2, 1)

    @pl.when(role == 1)
    def _():
        link[0] = link_of(1, 0)

    factor_step(work, 2)
    factor_step(work, 3)
    arrive(sent)
    for s in range(1, NZ):
        value = value + from_z[s]
    mine = pl.ds(pl.multiple_of(x * TALL + y * LOW, LOW), LOW)
    total[c, mine, :] = value
    sent = mail.spread("y", total.at[c, mine], total.at[c, mine])

    def role_copy(source, target, send, recv, to):
        return pltpu.make_async_remote_copy(
            src_ref=source, dst_ref=target, send_sem=role_send.at[send], recv_sem=role_recv.at[recv],
            device_id=device(y, x, c, z - role + to), device_id_type=MESH,
        )

    hands = {(2, 1): role_copy(hand.at[1], thin_in.at[0], 0, 0, 1),
             (2, 0): role_copy(hand.at[0], thin_in.at[1], 1, 1, 0),
             (1, 0): role_copy(hand.at[0], thin_in.at[2], 2, 2, 0)}
    gives = {(k, to): role_copy(solved.at[k], solved.at[k], 3 + 2 * k + n, 3 + k, to)
             for k in range(ROLES) for n, to in enumerate([t for t in range(ROLES) if t != k])}

    pick, lane = iota((16, 256), 0), iota((16, 256), 1)

    def solve(k, taken):
        at = (pick // PART == k) & (lane == c * 128 + x * 32 + pick % PART * 8 + y)
        value = at.astype(jnp.float32)
        for term in taken:
            value = value - term
        inverse = work[:, 256:]
        value = dot(dot(value, inverse, 1, 1), inverse)
        solved[k] = value
        return value

    def give(k):
        for to in range(ROLES):
            if to != k:
                gives[k, to].start()

    @pl.when(role == 2)
    def _():
        value = solve(2, [])
        hand[1] = dot(value, link[1])
        hands[2, 1].start()
        hand[0] = dot(value, link[0])
        hands[2, 0].start()
        give(2)

    @pl.when(role == 1)
    def _():
        hands[2, 1].wait_recv()
        value = solve(1, [thin_in[0]])
        hand[0] = dot(value, link[0])
        hands[1, 0].start()
        give(1)

    arrive(sent)
    sent = mail.spread("x", total.at[c, tall_at(x)], total.at[c, tall_at(x)])

    @pl.when(role == 0)
    def _():
        hands[2, 0].wait_recv()
        hands[1, 0].wait_recv()
        solve(0, [thin_in[1], thin_in[2]])
        give(0)

    arrive(sent)
    sent = [mail.send("c", 1, total.at[c], total.at[c])]
    for k in range(ROLES):

        @pl.when(role != k)
        def _():
            gives[k, (k + 1) % ROLES].wait_recv()

    arrive(sent)
    change = jnp.zeros((classes, 16), jnp.float32)
    for k in range(nblocks):
        for cc in range(NC):
            rows = total[cc, CLASS_ROWS * k : CLASS_ROWS * k + classes, :]
            change = change - dot(rows, solved[k, :, 128 * cc : 128 * cc + 128], 1, 1)
    out_ref[...] = coefs[...] + dot(change, owned)

    mail.close()

    @pl.when(role == 2)
    def _():
        hands[2, 1].wait_send()
        hands[2, 0].wait_send()

    @pl.when(role == 1)
    def _():
        hands[1, 0].wait_send()

    for k in range(ROLES):

        @pl.when(role == k)
        def _():
            for to in range(ROLES):
                if to != k:
                    gives[k, to].wait_send()


def body(points, targets, coefs, block_index):
    blocks, size = block_index.shape
    count, width = points.shape
    classes = targets.shape[1]
    f32 = jnp.float32
    out = pl.pallas_call(
        whole_body,
        out_shape=jax.ShapeDtypeStruct((classes, count), f32),
        in_specs=[ANY, ANY, ANY, SMEM, ANY],
        out_specs=VMEM,
        scratch_shapes=[
            pltpu.VMEM((128 * CHUNKS, count), f32),
            pltpu.VMEM((128 * CHUNKS, count), f32),
            pltpu.VMEM((classes, count), f32),
            pltpu.VMEM((classes, count), f32),
            pltpu.VMEM((classes, count), f32),
            pltpu.VMEM((blocks, size), jnp.int32),
            pltpu.VMEM((CHUNKS, 16, 128), f32),
            pltpu.VMEM((NZ, CHUNKS, 1, 128), f32),
            pltpu.VMEM((NC, CHUNKS, NX, blocks, PART, NY, 128), f32),
            pltpu.VMEM((PAD, 128), f32),
            pltpu.VMEM((NX, TALL, 128), f32),
            pltpu.VMEM((NY, LOW, 128), f32),
            pltpu.VMEM((NZ, LOW, 128), f32),
            pltpu.VMEM((TALL, 128), f32),
            pltpu.VMEM((LOW, 128), f32),
            pltpu.VMEM((NC, PAD, 128), f32),
            pltpu.VMEM((size, 2 * size), f32),
            pltpu.VMEM((2, size, size), f32),
            pltpu.VMEM((2, 16, size), f32),
            pltpu.VMEM((3, 16, size), f32),
            pltpu.VMEM((ROLES, 16, size), f32),
            pltpu.SemaphoreType.DMA((4,)),
            pltpu.SemaphoreType.DMA((COPIES,)),
            pltpu.SemaphoreType.DMA((COPIES,)),
            pltpu.SemaphoreType.DMA((9,)),
            pltpu.SemaphoreType.DMA((6,)),
        ],
        compiler_params=pltpu.CompilerParams(vmem_limit_bytes=56 << 20, collective_id=1, has_side_effects=True),
        name="block_updates",
    )(points.T, targets.T, coefs.T, block_index, block_index)
    return out.T


def solution(mesh):
    return jax.shard_map(
        body,
        mesh=mesh,
        in_specs=(
            P(("rows", "grp"), None),
            P(("rows", "grp"), None),
            P(("rows", "grp"), None),
            P(),
        ),
        out_specs=P(("rows", "grp"), None),
        check_vma=False,
    )
```

```python
import functools

import jax
import jax.numpy as jnp
from jax import lax
from jax.experimental import pallas as pl
from jax.experimental.pallas import tpu as pltpu
from jax.sharding import PartitionSpec as P

HIGH = lax.Precision.HIGHEST
VMEM = pl.BlockSpec(memory_space=pltpu.VMEM)
HBM = pl.BlockSpec(memory_space=pltpu.HBM)
MESH = pl.DeviceIdType.MESH
NY, NX, NC, NZ = 8, 4, 2, 12
PART = 4
CHUNKS = 4
PAD = 512
TALL, LOW = PAD // NX, PAD // NX // NY
CLASS_ROWS = 152
ROLES = 3
SPLIT = 3
ridge = 0.5


def dot(a, b, ca=1, cb=0):
    return lax.dot_general(a, b, (((ca,), (cb,)), ((), ())), precision=HIGH, preferred_element_type=jnp.float32)


def row_of(v, k):
    return jnp.broadcast_to(v[k:k + 1, :], v.shape)


def lane_of(v, k):
    return jnp.broadcast_to(v[:, k:k + 1], v.shape)


def eliminate(rows, t):
    place = lax.broadcasted_iota(jnp.int32, (8, 128), 0)
    top = rows[0]
    spread = [[lane_of(v, j) for j in range(8)] for v in rows[1:]]
    cols = [lane_of(top, j) for j in range(8)]
    forward = top
    full = top
    scale = jnp.zeros((8, 128), jnp.float32)
    for k in range(8):
        pivot = row_of(cols[k], k)
        inverse = 1.0 / pivot
        scale = jnp.where(place == k, inverse, scale)
        step = cols[k] * inverse
        both = jnp.where(place == k, 0.0, step)
        below = jnp.where(place > k, step, 0.0)
        for j in range(k + 1, 8):
            cols[j] = cols[j] - both * row_of(cols[j], k)
        forward = forward - below * row_of(forward, k)
        full = full - both * row_of(full, k)
    solved = full * scale
    done = forward * jnp.sqrt(scale)
    lines = [row_of(solved, j) for j in range(8)]
    out = []
    for p in range(1, 8):
        s = spread[p - 1]
        terms = [s[j] * lines[j] for j in range(8)]
        total = ((terms[0] + terms[1]) + (terms[2] + terms[3])) + ((terms[4] + terms[5]) + (terms[6] + terms[7]))
        live = jnp.where(t + p < 8, 1.0, 0.0).astype(jnp.float32)
        out.append(rows[p] - live * total)
    out.append(done)
    return [pltpu.roll(v, 120, 1) for v in out]


def factor_start(work, j):
    lo, hi = 64 * j, 64 * j + 64
    wide = jnp.concatenate([work[lo:hi, lo:hi], identity(64)], axis=1)
    return tuple(wide[8 * p : 8 * p + 8, :] for p in range(8))


def factor_groups(state, first, last):
    return lax.fori_loop(first, last, lambda t, state: tuple(eliminate(list(state), t)), state)


def factor_end(work, j, state):
    lo, hi = 64 * j, 64 * j + 64
    inverse = jnp.concatenate(state, axis=0)[:, :64]
    rows = dot(inverse, work[lo:hi, :])
    work[lo:hi, :] = rows
    if j < 3:
        work[hi:, :] = work[hi:, :] - dot(rows[:, hi:256], rows, 0, 0)


def iota(shape, axis):
    return lax.broadcasted_iota(jnp.int32, shape, axis)


def spot():
    line = lax.axis_index("rows")
    return line // (NX * NC), line // NC % NX, line % NC, lax.axis_index("grp")


def device(y, x, c, z):
    return ((y * NX + x) * NC + c, z)


def partner(axis, step):
    y, x, c, z = spot()
    if axis == "y":
        return device((y + step) % NY, x, c, z)
    if axis == "x":
        return device(y, (x + step) % NX, c, z)
    if axis == "z":
        return device(y, x, c, (z + step) % NZ)
    return device(y, x, (c + step) % NC, z)


SIZES = {"y": NY, "x": NX, "z": NZ, "c": NC}


def far_first(size):
    return sorted(range(1, size), key=lambda step: -min(step, size - step))


def greet():
    barrier = pltpu.get_barrier_semaphore()
    count = 0
    for axis, size in SIZES.items():
        for step in range(1, size):
            pl.semaphore_signal(barrier, inc=1, device_id=partner(axis, step), device_id_type=MESH)
            count += 1
    return count


class Mail:
    def __init__(self, send_sem, recv_sem):
        self.send_sem, self.recv_sem, self.used, self.sent = send_sem, recv_sem, 0, []

    def send(self, axis, step, source, target):
        copy = pltpu.make_async_remote_copy(
            src_ref=source,
            dst_ref=target,
            send_sem=self.send_sem.at[self.used],
            recv_sem=self.recv_sem.at[self.used],
            device_id=partner(axis, step),
            device_id_type=MESH,
        )
        copy.start()
        self.used += 1
        self.sent.append(copy)
        return copy

    def spread(self, axis, source, target):
        return [self.send(axis, step, source, target) for step in far_first(SIZES[axis])]

    def close(self):
        for copy in self.sent:
            copy.wait_send()


def arrive(copies):
    for copy in copies:
        copy.wait_recv()


COPIES = (
    2 + 2 * (NZ - 1) + 3 * (NX - 1 + NY - 1) + 1
    + (NX - 1) + (NY - 1) + (NZ - 1) + (NY - 1) + NY * (NX - 1) + NX
)


def half_rows(blocks_ref, c, k, lo=0, hi=CHUNKS):
    return jnp.concatenate([blocks_ref[c, ch, :, k].reshape(-1, 128) for ch in range(lo, hi)], axis=1)


def whole_rows(blocks_ref, k):
    return jnp.concatenate([half_rows(blocks_ref, c, k) for c in range(NC)], axis=0)


def kernel_block(left, right, width):
    cross = dot(left, right, 1, 1)
    left_sq = jnp.sum(left * left, axis=1, keepdims=True)
    right_sq = dot(jnp.ones((8, right.shape[1]), jnp.float32), right * right, 1, 1)[:1]
    return jnp.exp((left_sq + right_sq - 2.0 * cross) * (-2.0 / width))


def identity(size):
    return (iota((size, size), 0) == iota((size, size), 1)).astype(jnp.float32)


def factor_step(work, j):
    factor_end(work, j, factor_groups(factor_start(work, j), 0, 8))


def whole_body(
    pt_hbm, tt_hbm, ct_hbm, index_hbm, out_ref,
    index_ref, points, targets, coefs, index_rows, picked, landed, blocks,
    far, sums, from_x, from_y, from_z, sum_x, sum_y, total,
    work, link, solved,
    local_sem, send_sem, recv_sem, role_send, role_recv,
):
    y, x, c, z = spot()
    line = lax.axis_index("rows")
    me = line * NZ + z
    width, count = pt_hbm.shape
    classes = ct_hbm.shape[0]
    nblocks = index_hbm.shape[0]
    mail = Mail(send_sem, recv_sem)

    greeted = greet()
    loads = [
        pltpu.make_async_copy(index_hbm, index_ref, local_sem.at[0]),
        pltpu.make_async_copy(pt_hbm, points.at[pl.ds(0, width), pl.ds(0, count)], local_sem.at[1]),
        pltpu.make_async_copy(ct_hbm, coefs.at[:, pl.ds(0, count)], local_sem.at[2]),
        pltpu.make_async_copy(tt_hbm, targets, local_sem.at[3]),
        pltpu.make_async_copy(index_hbm, index_rows, local_sem.at[4]),
    ]
    for load in loads:
        load.start()
    points[width:, :] = jnp.zeros((points.shape[0] - width, 2 * count), jnp.float32)
    row_no = iota((16, count), 0)
    mine = jnp.full((16, count), -1, jnp.int32)
    loads[0].wait()
    for k in range(nblocks):
        for i in range(PART):
            mine = jnp.where(row_no == PART * k + i, index_ref[k, line * PART + i], mine)
    owned = (mine == iota((16, count), 1) + me * count).astype(jnp.float32)
    loads[1].wait()
    rows = dot(owned, points[:, :count], 1, 1)
    for ch in range(CHUNKS):
        picked[ch] = rows[:, 128 * ch : 128 * ch + 128]
    pl.semaphore_wait(pltpu.get_barrier_semaphore(), greeted)

    my_y = pl.ds(y, 1)
    first = [mail.send("z", s, picked.at[:, pl.ds((z + s) % NZ, 1)], landed.at[s]) for s in far_first(NZ)]
    loads[2].wait()
    pair = [mail.send("c", 1, points.at[pl.ds(0, width), pl.ds(0, count)], points.at[pl.ds(0, width), pl.ds(count, count)])]
    pair.append(mail.send("c", 1, coefs.at[:, pl.ds(0, count)], coefs.at[:, pl.ds(count, count)]))
    loads[3].wait()
    loads[4].wait()

    start = dot(targets[...] - ridge * coefs[:, :count], owned, 1, 1)
    sums[...] = jnp.zeros_like(sums)
    pick, lane = iota((16, 128), 0), iota((16, 128), 1)
    for k in range(nblocks):
        at = (pick // PART == k) & (lane == x * 32 + pick % PART * 8 + y)
        sums[CLASS_ROWS * k : CLASS_ROWS * k + classes, :] = -dot(start, at.astype(jnp.float32))

    arrive(first)
    row = picked[:, pl.ds(z, 1), :]
    for s in range(1, NZ):
        row = row + landed[s]
    my_k, my_i = z // PART, z % PART
    for ch in range(CHUNKS):
        blocks[c, ch, x, my_k, my_i, my_y, :] = row[ch]
    one = blocks.at[c, :, x, my_k, my_i, my_y]
    arrive(mail.spread("z", one, one))

    def along_y(lo, hi):
        some = blocks.at[c, lo:hi, x, :, :, my_y]
        return mail.spread("y", some, some)

    y0 = along_y(0, 2)
    some = blocks.at[c, 2, x, :, :, my_y]
    x1 = mail.spread("x", some, some)
    y2 = along_y(3, 4)
    arrive(x1)
    many = blocks.at[c, 2, :, :, :, my_y]
    y1 = mail.spread("y", many, many)
    arrive(y0)
    many = blocks.at[c, 0:2, x]
    x0 = mail.spread("x", many, many)
    arrive(y2)
    many = blocks.at[c, 3, x]
    x2 = mail.spread("x", many, many)

    arrive(pair)
    points_sq = jnp.sum(points[...] * points[...], axis=0, keepdims=True)

    def cross_part(lo):
        half = jnp.concatenate([half_rows(blocks, c, k, lo, lo + 2) for k in range(nblocks)], axis=0)
        squares = jnp.sum(half * half, axis=1, keepdims=True)
        return squares - 2.0 * dot(half, points[128 * lo : 128 * lo + 256, :])

    arrive(x0)
    far[...] = cross_part(0) + points_sq
    arrive(y1)
    arrive(x2)
    other = [mail.send("c", 1, blocks.at[c], blocks.at[c])]
    kern = jnp.exp((far[...] + cross_part(2)) * (-2.0 / width))
    term = dot(coefs[...], kern, 1, 1)
    for k in range(nblocks):
        at = slice(CLASS_ROWS * k, CLASS_ROWS * k + classes)
        sums[at, :] = sums[at, :] + term[:, 128 * k : 128 * k + 128]

    def tall_at(x):
        return pl.ds(pl.multiple_of(x * TALL, TALL), TALL)

    def low_at(y):
        return pl.ds(pl.multiple_of(y * LOW, LOW), LOW)

    sent = [mail.send("x", s, sums.at[tall_at((x + s) % NX)], from_x.at[s]) for s in far_first(NX)]
    role = z % ROLES
    arrive(other)
    own = whole_rows(blocks, role)
    work[:, 256:] = identity(256)
    work[:, :256] = kernel_block(own, own, width) + ridge * identity(256)
    state = factor_groups(factor_start(work, 0), 0, SPLIT)
    arrive(sent)
    value = sums[tall_at(x)]
    for s in range(1, NX):
        value = value + from_x[s]
    sum_x[...] = value
    sent = [mail.send("y", s, sum_x.at[low_at((y + s) % NY)], from_y.at[s]) for s in far_first(NY)]
    factor_end(work, 0, factor_groups(state, SPLIT, 8))
    factor_step(work, 1)
    arrive(sent)
    value = sum_x[low_at(y)]
    for s in range(1, NY):
        value = value + from_y[s]
    sum_y[...] = value
    sent = [mail.send("z", s, sum_y, from_z.at[s]) for s in far_first(NZ)]

    factor_step(work, 2)
    factor_step(work, 3)
    arrive(sent)
    for s in range(1, NZ):
        value = value + from_z[s]
    def piece_of(y):
        return total.at[c, pl.ds(pl.multiple_of(x * TALL + y * LOW, LOW), LOW)]

    mine = piece_of(y)
    mine[...] = value
    down = {s: mail.send("y", s, mine, mine) for s in far_first(NY)}
    across = mail.spread("x", mine, mine)

    gives = {}
    for k in range(ROLES):
        for n, to in enumerate([to for to in range(ROLES) if to != k]):
            gives[k, to] = pltpu.make_async_remote_copy(
                src_ref=solved.at[k],
                dst_ref=solved.at[k],
                send_sem=role_send.at[2 * k + n],
                recv_sem=role_recv.at[k],
                device_id=device(y, x, c, z - role + to),
                device_id_type=MESH,
            )

    def give(k):
        for to in range(ROLES):
            if to != k:
                gives[k, to].start()

    def through(value):
        inverse = work[:, 256:]
        return dot(dot(value, inverse, 1, 1), inverse)

    def own_pick(k):
        pick, lane = iota((16, 256), 0), iota((16, 256), 1)
        at = (pick // PART == k) & (lane == c * 128 + x * 32 + pick % PART * 8 + y)
        return at.astype(jnp.float32)

    def links(j):
        lane, at = iota((256, 256), 1), iota((256, 256), 0)
        line_of = (lane % 8 * NX + lane // 32 % 4) * NC + lane // 128
        order = (at == line_of * PART + lane // 8 % 4).astype(jnp.float32)
        numbers = dot(index_rows[...].astype(jnp.float32), order)
        for n, k in enumerate(range(j + 1, nblocks)):
            column = jnp.sum(jnp.where(at == lane, numbers[k : k + 1, :], 0.0), axis=1, keepdims=True)
            same = (column == numbers[j : j + 1, :]).astype(jnp.float32)
            link[n] = kernel_block(whole_rows(blocks, k), whole_rows(blocks, j), width) + ridge * same

    @pl.when(role == 2)
    def _():
        solved[2] = through(own_pick(2))
        give(2)

    @pl.when(role == 1)
    def _():
        links(1)
        link[0] = through(link[0])
        solved[1] = through(own_pick(1))

    @pl.when(role == 0)
    def _():
        links(0)

    def forward(s):
        arrive([down[s]])
        piece = piece_of((y - s + NY) % NY)
        return mail.spread("x", piece, piece)

    near_first = list(reversed(far_first(NY)))
    for s in near_first[:4]:
        across += forward(s)

    @pl.when(role == 1)
    def _():
        gives[2, 1].wait_recv()
        solved[1] = solved[1] - dot(solved[2], link[0])
        give(1)

    for s in near_first[4:]:
        across += forward(s)

    @pl.when(role == 0)
    def _():
        gives[2, 0].wait_recv()
        value = own_pick(0) - dot(solved[2], link[1])
        gives[1, 0].wait_recv()
        solved[0] = through(value - dot(solved[1], link[0]))
        give(0)

    tall = total.at[c, tall_at(x)]
    sent = [mail.send("c", 1, tall, tall)]

    arrive(across)
    for s in range(1, NX):
        tall = total.at[c, tall_at((x + s) % NX)]
        sent.append(mail.send("c", 1, tall, tall))
    @pl.when(role == 2)
    def _():
        gives[1, 2].wait_recv()

    @pl.when(role != 0)
    def _():
        gives[0, 1].wait_recv()

    def change_of(cc):
        change = jnp.zeros((classes, 16), jnp.float32)
        for k in range(nblocks):
            rows = total[cc, CLASS_ROWS * k : CLASS_ROWS * k + classes, :]
            at = pl.ds(pl.multiple_of(cc * 128, 128), 128)
            change = change - dot(rows, solved[k, :, at], 1, 1)
        return change

    change = change_of(c)
    arrive(sent)
    change = change + change_of(1 - c)
    out_ref[...] = coefs[:, :count] + dot(change, owned)

    mail.close()

    for k in range(ROLES):

        @pl.when(role == k)
        def _():
            for to in range(ROLES):
                if to != k:
                    gives[k, to].wait_send()


def body(points, targets, coefs, block_index):
    blocks, size = block_index.shape
    count, width = points.shape
    classes = targets.shape[1]
    f32 = jnp.float32
    out = pl.pallas_call(
        whole_body,
        out_shape=jax.ShapeDtypeStruct((classes, count), f32),
        in_specs=[HBM] * 4,
        out_specs=VMEM,
        scratch_shapes=[
            pltpu.SMEM((blocks, size), jnp.int32),
            pltpu.VMEM((128 * CHUNKS, 2 * count), f32),
            pltpu.VMEM((classes, count), f32),
            pltpu.VMEM((classes, 2 * count), f32),
            pltpu.VMEM((blocks, size), jnp.int32),
            pltpu.VMEM((CHUNKS, 16, 128), f32),
            pltpu.VMEM((NZ, CHUNKS, 1, 128), f32),
            pltpu.VMEM((NC, CHUNKS, NX, blocks, PART, NY, 128), f32),
            pltpu.VMEM((blocks * size // 2, 2 * count), f32),
            pltpu.VMEM((PAD, 128), f32),
            pltpu.VMEM((NX, TALL, 128), f32),
            pltpu.VMEM((NY, LOW, 128), f32),
            pltpu.VMEM((NZ, LOW, 128), f32),
            pltpu.VMEM((TALL, 128), f32),
            pltpu.VMEM((LOW, 128), f32),
            pltpu.VMEM((NC, PAD, 128), f32),
            pltpu.VMEM((size, 2 * size), f32),
            pltpu.VMEM((2, size, size), f32),
            pltpu.VMEM((ROLES, 16, size), f32),
            pltpu.SemaphoreType.DMA((5,)),
            pltpu.SemaphoreType.DMA((COPIES,)),
            pltpu.SemaphoreType.DMA((COPIES,)),
            pltpu.SemaphoreType.DMA((2 * ROLES,)),
            pltpu.SemaphoreType.DMA((ROLES,)),
        ],
        compiler_params=pltpu.CompilerParams(vmem_limit_bytes=56307712, collective_id=1, has_side_effects=True),
        name="block_updates",
    )(points.T, targets.T, coefs.T, block_index)
    return out.T


def solution(mesh):
    return jax.shard_map(
        body,
        mesh=mesh,
        in_specs=(
            P(("rows", "grp"), None),
            P(("rows", "grp"), None),
            P(("rows", "grp"), None),
            P(),
        ),
        out_specs=P(("rows", "grp"), None),
        check_vma=False,
    )
```

```python
import functools

import jax
import jax.numpy as jnp
from jax import lax
from jax.experimental import pallas as pl
from jax.experimental.pallas import tpu as pltpu
from jax.sharding import PartitionSpec as P

HIGH = lax.Precision.HIGHEST
VMEM = pl.BlockSpec(memory_space=pltpu.VMEM)
HBM = pl.BlockSpec(memory_space=pltpu.HBM)
MESH = pl.DeviceIdType.MESH
NY, NX, NC, NZ = 8, 4, 2, 12
PART = 4
CHUNKS = 4
PAD = 448
TALL, LOW = PAD // NX, PAD // NX // NY
CLASS_ROWS = 147
ROLES = 3
SPLIT = 3
ridge = 0.5


def dot(a, b, ca=1, cb=0):
    return lax.dot_general(a, b, (((ca,), (cb,)), ((), ())), precision=HIGH, preferred_element_type=jnp.float32)


def row_of(v, k):
    return jnp.broadcast_to(v[k:k + 1, :], v.shape)


def lane_of(v, k):
    return jnp.broadcast_to(v[:, k:k + 1], v.shape)


def eliminate(rows, t):
    place = lax.broadcasted_iota(jnp.int32, (8, 128), 0)
    top = rows[0]
    spread = [[lane_of(v, j) for j in range(8)] for v in rows[1:]]
    cols = [lane_of(top, j) for j in range(8)]
    forward = top
    full = top
    scale = jnp.zeros((8, 128), jnp.float32)
    for k in range(8):
        pivot = row_of(cols[k], k)
        inverse = 1.0 / pivot
        scale = jnp.where(place == k, inverse, scale)
        step = cols[k] * inverse
        both = jnp.where(place == k, 0.0, step)
        below = jnp.where(place > k, step, 0.0)
        for j in range(k + 1, 8):
            cols[j] = cols[j] - both * row_of(cols[j], k)
        forward = forward - below * row_of(forward, k)
        full = full - both * row_of(full, k)
    solved = full * scale
    done = forward * jnp.sqrt(scale)
    lines = [row_of(solved, j) for j in range(8)]
    out = []
    for p in range(1, 8):
        s = spread[p - 1]
        terms = [s[j] * lines[j] for j in range(8)]
        total = ((terms[0] + terms[1]) + (terms[2] + terms[3])) + ((terms[4] + terms[5]) + (terms[6] + terms[7]))
        live = jnp.where(t + p < 8, 1.0, 0.0).astype(jnp.float32)
        out.append(rows[p] - live * total)
    out.append(done)
    return [pltpu.roll(v, 120, 1) for v in out]


def factor_start(work, j):
    lo, hi = 64 * j, 64 * j + 64
    wide = jnp.concatenate([work[lo:hi, lo:hi], identity(64)], axis=1)
    return tuple(wide[8 * p : 8 * p + 8, :] for p in range(8))


def factor_groups(state, first, last):
    return lax.fori_loop(first, last, lambda t, state: tuple(eliminate(list(state), t)), state)


def factor_end(work, j, state):
    lo, hi = 64 * j, 64 * j + 64
    inverse = jnp.concatenate(state, axis=0)[:, :64]
    rows = dot(inverse, work[lo:hi, :])
    work[lo:hi, :] = rows
    if j < 3:
        work[hi:, :] = work[hi:, :] - dot(rows[:, hi:256], rows, 0, 0)


def iota(shape, axis):
    return lax.broadcasted_iota(jnp.int32, shape, axis)


def spot():
    line = lax.axis_index("rows")
    return line // (NX * NC), line // NC % NX, line % NC, lax.axis_index("grp")


def device(y, x, c, z):
    return ((y * NX + x) * NC + c, z)


def partner(axis, step):
    y, x, c, z = spot()
    if axis == "y":
        return device((y + step) % NY, x, c, z)
    if axis == "x":
        return device(y, (x + step) % NX, c, z)
    if axis == "z":
        return device(y, x, c, (z + step) % NZ)
    return device(y, x, (c + step) % NC, z)


SIZES = {"y": NY, "x": NX, "z": NZ, "c": NC}


def far_first(size):
    return sorted(range(1, size), key=lambda step: -min(step, size - step))


def greet():
    barrier = pltpu.get_barrier_semaphore()
    count = 0
    for axis, size in SIZES.items():
        for step in range(1, size):
            pl.semaphore_signal(barrier, inc=1, device_id=partner(axis, step), device_id_type=MESH)
            count += 1
    return count


class Mail:
    def __init__(self, send_sem, recv_sem):
        self.send_sem, self.recv_sem, self.used, self.sent = send_sem, recv_sem, 0, []

    def send(self, axis, step, source, target):
        copy = pltpu.make_async_remote_copy(
            src_ref=source,
            dst_ref=target,
            send_sem=self.send_sem.at[self.used],
            recv_sem=self.recv_sem.at[self.used],
            device_id=partner(axis, step),
            device_id_type=MESH,
        )
        copy.start()
        self.used += 1
        self.sent.append(copy)
        return copy

    def spread(self, axis, source, target):
        return [self.send(axis, step, source, target) for step in far_first(SIZES[axis])]

    def close(self):
        for copy in self.sent:
            copy.wait_send()


def arrive(copies):
    for copy in copies:
        copy.wait_recv()


COPIES = (
    2 + 2 * (NZ - 1) + 3 * (NX - 1 + NY - 1) + 1
    + (NX - 1) + (NY - 1) + (NZ - 1) + (NY - 1) + NY * (NX - 1) + NX
)


def half_rows(blocks_ref, c, k, lo=0, hi=CHUNKS):
    return jnp.concatenate([blocks_ref[c, ch, :, k].reshape(-1, 128) for ch in range(lo, hi)], axis=1)


def whole_rows(blocks_ref, k):
    return jnp.concatenate([half_rows(blocks_ref, c, k) for c in range(NC)], axis=0)


def kernel_block(left, right, width):
    cross = dot(left, right, 1, 1)
    left_sq = jnp.sum(left * left, axis=1, keepdims=True)
    right_sq = dot(jnp.ones((8, right.shape[1]), jnp.float32), right * right, 1, 1)[:1]
    return jnp.exp((left_sq + right_sq - 2.0 * cross) * (-2.0 / width))


def identity(size):
    return (iota((size, size), 0) == iota((size, size), 1)).astype(jnp.float32)


def factor_step(work, j):
    factor_end(work, j, factor_groups(factor_start(work, j), 0, 8))


def whole_body(
    pt_hbm, tt_hbm, ct_hbm, index_hbm, out_ref,
    index_ref, points, targets, coefs, index_rows, picked, landed, blocks,
    far, sums, from_x, from_y, from_z, sum_x, sum_y, total,
    work, link, solved,
    local_sem, send_sem, recv_sem, role_send, role_recv,
):
    y, x, c, z = spot()
    line = lax.axis_index("rows")
    me = line * NZ + z
    width, count = pt_hbm.shape
    classes = ct_hbm.shape[0]
    nblocks = index_hbm.shape[0]
    mail = Mail(send_sem, recv_sem)

    greeted = greet()
    loads = [
        pltpu.make_async_copy(index_hbm, index_ref, local_sem.at[0]),
        pltpu.make_async_copy(pt_hbm, points.at[pl.ds(0, width), pl.ds(0, count)], local_sem.at[1]),
        pltpu.make_async_copy(ct_hbm, coefs.at[:, pl.ds(0, count)], local_sem.at[2]),
        pltpu.make_async_copy(tt_hbm, targets, local_sem.at[3]),
        pltpu.make_async_copy(index_hbm, index_rows, local_sem.at[4]),
    ]
    for load in loads:
        load.start()
    points[width:, :] = jnp.zeros((points.shape[0] - width, 2 * count), jnp.float32)
    row_no = iota((16, count), 0)
    mine = jnp.full((16, count), -1, jnp.int32)
    loads[0].wait()
    for k in range(nblocks):
        for i in range(PART):
            mine = jnp.where(row_no == PART * k + i, index_ref[k, line * PART + i], mine)
    owned = (mine == iota((16, count), 1) + me * count).astype(jnp.float32)
    loads[1].wait()
    rows = dot(owned, points[:, :count], 1, 1)
    for ch in range(CHUNKS):
        picked[ch] = rows[:, 128 * ch : 128 * ch + 128]
    pl.semaphore_wait(pltpu.get_barrier_semaphore(), greeted)

    my_y = pl.ds(y, 1)
    first = [mail.send("z", s, picked.at[:, pl.ds((z + s) % NZ, 1)], landed.at[s]) for s in far_first(NZ)]
    loads[2].wait()
    pair = [mail.send("c", 1, points.at[pl.ds(0, width), pl.ds(0, count)], points.at[pl.ds(0, width), pl.ds(count, count)])]
    pair.append(mail.send("c", 1, coefs.at[:, pl.ds(0, count)], coefs.at[:, pl.ds(count, count)]))
    loads[3].wait()
    loads[4].wait()

    start = dot(targets[...] - ridge * coefs[:, :count], owned, 1, 1)
    sums[...] = jnp.zeros_like(sums)
    pick, lane = iota((16, 128), 0), iota((16, 128), 1)
    for k in range(nblocks):
        at = (pick // PART == k) & (lane == x * 32 + pick % PART * 8 + y)
        sums[CLASS_ROWS * k : CLASS_ROWS * k + classes, :] = -dot(start, at.astype(jnp.float32))

    arrive(first)
    row = picked[:, pl.ds(z, 1), :]
    for s in range(1, NZ):
        row = row + landed[s]
    my_k, my_i = z // PART, z % PART
    for ch in range(CHUNKS):
        blocks[c, ch, x, my_k, my_i, my_y, :] = row[ch]
    one = blocks.at[c, :, x, my_k, my_i, my_y]
    arrive(mail.spread("z", one, one))

    def along_y(lo, hi):
        some = blocks.at[c, lo:hi, x, :, :, my_y]
        return mail.spread("y", some, some)

    y0 = along_y(0, 2)
    some = blocks.at[c, 2:4, x, :, :, my_y]
    x1 = mail.spread("x", some, some)
    arrive(x1)
    many = blocks.at[c, 2:4, :, :, :, my_y]
    y1 = mail.spread("y", many, many)
    arrive(y0)
    many = blocks.at[c, 0:2, x]
    x0 = mail.spread("x", many, many)

    arrive(pair)
    points_sq = jnp.sum(points[...] * points[...], axis=0, keepdims=True)

    def cross_part(lo):
        half = jnp.concatenate([half_rows(blocks, c, k, lo, lo + 2) for k in range(nblocks)], axis=0)
        squares = jnp.sum(half * half, axis=1, keepdims=True)
        return squares - 2.0 * dot(half, points[128 * lo : 128 * lo + 256, :])

    arrive(x0)
    far[...] = cross_part(0) + points_sq
    arrive(y1)
    other = [mail.send("c", 1, blocks.at[c], blocks.at[c])]
    kern = jnp.exp((far[...] + cross_part(2)) * (-2.0 / width))
    term = dot(coefs[...], kern, 1, 1)
    for k in range(nblocks):
        at = slice(CLASS_ROWS * k, CLASS_ROWS * k + classes)
        sums[at, :] = sums[at, :] + term[:, 128 * k : 128 * k + 128]

    def tall_at(x):
        return pl.ds(pl.multiple_of(x * TALL, TALL), TALL)

    def low_at(y):
        return pl.ds(pl.multiple_of(y * LOW, LOW), LOW)

    sent = [mail.send("x", s, sums.at[tall_at((x + s) % NX)], from_x.at[s]) for s in far_first(NX)]
    role = z % ROLES
    arrive(other)
    own = whole_rows(blocks, role)
    work[:, 256:] = identity(256)
    work[:, :256] = kernel_block(own, own, width) + ridge * identity(256)
    state = factor_groups(factor_start(work, 0), 0, SPLIT)
    arrive(sent)
    value = sums[tall_at(x)]
    for s in range(1, NX):
        value = value + from_x[s]
    sum_x[...] = value
    sent = [mail.send("y", s, sum_x.at[low_at((y + s) % NY)], from_y.at[s]) for s in far_first(NY)]
    factor_end(work, 0, factor_groups(state, SPLIT, 8))
    factor_step(work, 1)
    arrive(sent)
    value = sum_x[low_at(y)]
    for s in range(1, NY):
        value = value + from_y[s]
    sum_y[...] = value
    sent = [mail.send("z", s, sum_y, from_z.at[s]) for s in far_first(NZ)]

    factor_step(work, 2)
    factor_step(work, 3)
    arrive(sent)
    for s in range(1, NZ):
        value = value + from_z[s]
    def piece_of(y):
        return total.at[c, pl.ds(pl.multiple_of(x * TALL + y * LOW, LOW), LOW)]

    mine = piece_of(y)
    mine[...] = value
    down = {s: mail.send("y", s, mine, mine) for s in far_first(NY)}
    across = mail.spread("x", mine, mine)

    gives = {}
    for k in range(ROLES):
        for n, to in enumerate([to for to in range(ROLES) if to != k]):
            gives[k, to] = pltpu.make_async_remote_copy(
                src_ref=solved.at[k],
                dst_ref=solved.at[k],
                send_sem=role_send.at[2 * k + n],
                recv_sem=role_recv.at[k],
                device_id=device(y, x, c, z - role + to),
                device_id_type=MESH,
            )

    def give(k):
        for to in range(ROLES):
            if to != k:
                gives[k, to].start()

    def through(value):
        inverse = work[:, 256:]
        return dot(dot(value, inverse, 1, 1), inverse)

    def own_pick(k):
        pick, lane = iota((16, 256), 0), iota((16, 256), 1)
        at = (pick // PART == k) & (lane == c * 128 + x * 32 + pick % PART * 8 + y)
        return at.astype(jnp.float32)

    def links(j):
        lane, at = iota((256, 256), 1), iota((256, 256), 0)
        line_of = (lane % 8 * NX + lane // 32 % 4) * NC + lane // 128
        order = (at == line_of * PART + lane // 8 % 4).astype(jnp.float32)
        numbers = dot(index_rows[...].astype(jnp.float32), order)
        for n, k in enumerate(range(j + 1, nblocks)):
            column = jnp.sum(jnp.where(at == lane, numbers[k : k + 1, :], 0.0), axis=1, keepdims=True)
            same = (column == numbers[j : j + 1, :]).astype(jnp.float32)
            link[n] = kernel_block(whole_rows(blocks, k), whole_rows(blocks, j), width) + ridge * same

    @pl.when(role == 2)
    def _():
        solved[2] = through(own_pick(2))
        give(2)

    @pl.when(role == 1)
    def _():
        links(1)
        link[0] = through(link[0])
        solved[1] = through(own_pick(1))

    @pl.when(role == 0)
    def _():
        links(0)

    def forward(s):
        arrive([down[s]])
        piece = piece_of((y - s + NY) % NY)
        return mail.spread("x", piece, piece)

    near_first = list(reversed(far_first(NY)))
    for s in near_first[:4]:
        across += forward(s)

    @pl.when(role == 1)
    def _():
        gives[2, 1].wait_recv()
        solved[1] = solved[1] - dot(solved[2], link[0])
        give(1)

    for s in near_first[4:]:
        across += forward(s)

    @pl.when(role == 0)
    def _():
        gives[2, 0].wait_recv()
        value = own_pick(0) - dot(solved[2], link[1])
        gives[1, 0].wait_recv()
        solved[0] = through(value - dot(solved[1], link[0]))
        give(0)

    tall = total.at[c, tall_at(x)]
    sent = [mail.send("c", 1, tall, tall)]

    near = list(reversed(far_first(NX)))
    for n, s in enumerate(near):
        arrive(across[len(near) - 1 - n :: len(near)])
        tall = total.at[c, tall_at((x - s + NX) % NX)]
        sent.append(mail.send("c", 1, tall, tall))
    @pl.when(role == 2)
    def _():
        gives[1, 2].wait_recv()

    @pl.when(role != 0)
    def _():
        gives[0, 1].wait_recv()

    def change_of(cc):
        change = jnp.zeros((classes, 16), jnp.float32)
        for k in range(nblocks):
            rows = total[cc, CLASS_ROWS * k : CLASS_ROWS * k + classes, :]
            at = pl.ds(pl.multiple_of(cc * 128, 128), 128)
            change = change - dot(rows, solved[k, :, at], 1, 1)
        return change

    change = change_of(c)
    arrive(sent)
    change = change + change_of(1 - c)
    out_ref[...] = coefs[:, :count] + dot(change, owned)

    mail.close()

    for k in range(ROLES):

        @pl.when(role == k)
        def _():
            for to in range(ROLES):
                if to != k:
                    gives[k, to].wait_send()


def body(points, targets, coefs, block_index):
    blocks, size = block_index.shape
    count, width = points.shape
    classes = targets.shape[1]
    f32 = jnp.float32
    out = pl.pallas_call(
        whole_body,
        out_shape=jax.ShapeDtypeStruct((classes, count), f32),
        in_specs=[HBM] * 4,
        out_specs=VMEM,
        scratch_shapes=[
            pltpu.SMEM((blocks, size), jnp.int32),
            pltpu.VMEM((128 * CHUNKS, 2 * count), f32),
            pltpu.VMEM((classes, count), f32),
            pltpu.VMEM((classes, 2 * count), f32),
            pltpu.VMEM((blocks, size), jnp.int32),
            pltpu.VMEM((CHUNKS, 16, 128), f32),
            pltpu.VMEM((NZ, CHUNKS, 1, 128), f32),
            pltpu.VMEM((NC, CHUNKS, NX, blocks, PART, NY, 128), f32),
            pltpu.VMEM((blocks * size // 2, 2 * count), f32),
            pltpu.VMEM((PAD, 128), f32),
            pltpu.VMEM((NX, TALL, 128), f32),
            pltpu.VMEM((NY, LOW, 128), f32),
            pltpu.VMEM((NZ, LOW, 128), f32),
            pltpu.VMEM((TALL, 128), f32),
            pltpu.VMEM((LOW, 128), f32),
            pltpu.VMEM((NC, PAD, 128), f32),
            pltpu.VMEM((size, 2 * size), f32),
            pltpu.VMEM((2, size, size), f32),
            pltpu.VMEM((ROLES, 16, size), f32),
            pltpu.SemaphoreType.DMA((5,)),
            pltpu.SemaphoreType.DMA((COPIES,)),
            pltpu.SemaphoreType.DMA((COPIES,)),
            pltpu.SemaphoreType.DMA((2 * ROLES,)),
            pltpu.SemaphoreType.DMA((ROLES,)),
        ],
        compiler_params=pltpu.CompilerParams(vmem_limit_bytes=56307712, collective_id=1, has_side_effects=True),
        name="block_updates",
    )(points.T, targets.T, coefs.T, block_index)
    return out.T


def solution(mesh):
    return jax.shard_map(
        body,
        mesh=mesh,
        in_specs=(
            P(("rows", "grp"), None),
            P(("rows", "grp"), None),
            P(("rows", "grp"), None),
            P(),
        ),
        out_specs=P(("rows", "grp"), None),
        check_vma=False,
    )
```

```python
import functools

import jax
import jax.numpy as jnp
from jax import lax
from jax.experimental import pallas as pl
from jax.experimental.pallas import tpu as pltpu
from jax.sharding import PartitionSpec as P

HIGH = lax.Precision.HIGHEST
VMEM = pl.BlockSpec(memory_space=pltpu.VMEM)
HBM = pl.BlockSpec(memory_space=pltpu.HBM)
MESH = pl.DeviceIdType.MESH
NY, NX, NC, NZ = 8, 4, 2, 12
PART = 4
CHUNKS = 4
PAD = 448
TALL, LOW = PAD // NX, PAD // NX // NY
CLASS_ROWS = 147
ROLES = 3
SPLIT = 3
ridge = 0.5


def dot(a, b, ca=1, cb=0):
    return lax.dot_general(a, b, (((ca,), (cb,)), ((), ())), precision=HIGH, preferred_element_type=jnp.float32)


def row_of(v, k):
    return jnp.broadcast_to(v[k:k + 1, :], v.shape)


def lane_of(v, k):
    return jnp.broadcast_to(v[:, k:k + 1], v.shape)


def eliminate(rows, t):
    place = lax.broadcasted_iota(jnp.int32, (8, 128), 0)
    top = rows[0]
    spread = [[lane_of(v, j) for j in range(8)] for v in rows[1:]]
    cols = [lane_of(top, j) for j in range(8)]
    forward = top
    full = top
    scale = jnp.zeros((8, 128), jnp.float32)
    for k in range(8):
        pivot = row_of(cols[k], k)
        inverse = 1.0 / pivot
        scale = jnp.where(place == k, inverse, scale)
        step = cols[k] * inverse
        both = jnp.where(place == k, 0.0, step)
        below = jnp.where(place > k, step, 0.0)
        for j in range(k + 1, 8):
            cols[j] = cols[j] - both * row_of(cols[j], k)
        forward = forward - below * row_of(forward, k)
        full = full - both * row_of(full, k)
    solved = full * scale
    done = forward * jnp.sqrt(scale)
    lines = [row_of(solved, j) for j in range(8)]
    out = []
    for p in range(1, 8):
        s = spread[p - 1]
        terms = [s[j] * lines[j] for j in range(8)]
        total = ((terms[0] + terms[1]) + (terms[2] + terms[3])) + ((terms[4] + terms[5]) + (terms[6] + terms[7]))
        live = jnp.where(t + p < 8, 1.0, 0.0).astype(jnp.float32)
        out.append(rows[p] - live * total)
    out.append(done)
    return [pltpu.roll(v, 120, 1) for v in out]


def factor_start(work, j):
    lo, hi = 64 * j, 64 * j + 64
    wide = jnp.concatenate([work[lo:hi, lo:hi], identity(64)], axis=1)
    return tuple(wide[8 * p : 8 * p + 8, :] for p in range(8))


def factor_groups(state, first, last):
    return lax.fori_loop(first, last, lambda t, state: tuple(eliminate(list(state), t)), state)


def factor_end(work, j, state):
    lo, hi = 64 * j, 64 * j + 64
    inverse = jnp.concatenate(state, axis=0)[:, :64]
    rows = dot(inverse, work[lo:hi, :])
    work[lo:hi, :] = rows
    if j < 3:
        work[hi:, :] = work[hi:, :] - dot(rows[:, hi:256], rows, 0, 0)


def iota(shape, axis):
    return lax.broadcasted_iota(jnp.int32, shape, axis)


def spot():
    line = lax.axis_index("rows")
    return line // (NX * NC), line // NC % NX, line % NC, lax.axis_index("grp")


def device(y, x, c, z):
    return ((y * NX + x) * NC + c, z)


def partner(axis, step):
    y, x, c, z = spot()
    if axis == "y":
        return device((y + step) % NY, x, c, z)
    if axis == "x":
        return device(y, (x + step) % NX, c, z)
    if axis == "z":
        return device(y, x, c, (z + step) % NZ)
    return device(y, x, (c + step) % NC, z)


SIZES = {"z": NZ, "y": NY, "x": NX, "c": NC}


def far_first(size):
    return sorted(range(1, size), key=lambda step: -min(step, size - step))


def greet():
    barrier = pltpu.get_barrier_semaphore()
    count = 0
    for axis, size in SIZES.items():
        for step in far_first(size):
            pl.semaphore_signal(barrier, inc=1, device_id=partner(axis, step), device_id_type=MESH)
            count += 1
    return count


class Mail:
    def __init__(self, send_sem, recv_sem):
        self.send_sem, self.recv_sem, self.used, self.sent = send_sem, recv_sem, 0, []

    def send(self, axis, step, source, target):
        copy = pltpu.make_async_remote_copy(
            src_ref=source,
            dst_ref=target,
            send_sem=self.send_sem.at[self.used],
            recv_sem=self.recv_sem.at[self.used],
            device_id=partner(axis, step),
            device_id_type=MESH,
        )
        copy.start()
        self.used += 1
        self.sent.append(copy)
        return copy

    def spread(self, axis, source, target):
        return [self.send(axis, step, source, target) for step in far_first(SIZES[axis])]

    def close(self):
        for copy in self.sent:
            copy.wait_send()


def arrive(copies):
    for copy in copies:
        copy.wait_recv()


COPIES = (
    2 + 2 * (NZ - 1) + 3 * (NX - 1 + NY - 1) + 1
    + (NX - 1) + (NY - 1) + (NZ - 1) + (NY - 1) + NY * (NX - 1) + NX
)


def half_rows(blocks_ref, c, k, lo=0, hi=CHUNKS):
    return jnp.concatenate([blocks_ref[c, ch, :, k].reshape(-1, 128) for ch in range(lo, hi)], axis=1)


def whole_rows(blocks_ref, k):
    return jnp.concatenate([half_rows(blocks_ref, c, k) for c in range(NC)], axis=0)


def kernel_block(left, right, width):
    cross = dot(left, right, 1, 1)
    left_sq = jnp.sum(left * left, axis=1, keepdims=True)
    right_sq = dot(jnp.ones((8, right.shape[1]), jnp.float32), right * right, 1, 1)[:1]
    return jnp.exp((left_sq + right_sq - 2.0 * cross) * (-2.0 / width))


def identity(size):
    return (iota((size, size), 0) == iota((size, size), 1)).astype(jnp.float32)


def factor_step(work, j):
    factor_end(work, j, factor_groups(factor_start(work, j), 0, 8))


def whole_body(
    pt_hbm, tt_hbm, ct_hbm, index_hbm, out_ref,
    index_ref, points, targets, coefs, index_rows, picked, landed, blocks,
    far, sums, from_x, from_y, from_z, sum_x, sum_y, total,
    work, link, solved,
    local_sem, send_sem, recv_sem, role_send, role_recv,
):
    y, x, c, z = spot()
    line = lax.axis_index("rows")
    me = line * NZ + z
    width, count = pt_hbm.shape
    classes = ct_hbm.shape[0]
    nblocks = index_hbm.shape[0]
    mail = Mail(send_sem, recv_sem)

    greeted = greet()
    loads = [
        pltpu.make_async_copy(index_hbm, index_ref, local_sem.at[0]),
        pltpu.make_async_copy(pt_hbm, points.at[pl.ds(0, width), pl.ds(0, count)], local_sem.at[1]),
        pltpu.make_async_copy(ct_hbm, coefs.at[:, pl.ds(0, count)], local_sem.at[2]),
        pltpu.make_async_copy(tt_hbm, targets, local_sem.at[3]),
        pltpu.make_async_copy(index_hbm, index_rows, local_sem.at[4]),
    ]
    for load in loads:
        load.start()
    points[width:, :] = jnp.zeros((points.shape[0] - width, 2 * count), jnp.float32)
    row_no = iota((16, count), 0)
    mine = jnp.full((16, count), -1, jnp.int32)
    loads[0].wait()
    for k in range(nblocks):
        for i in range(PART):
            mine = jnp.where(row_no == PART * k + i, index_ref[k, line * PART + i], mine)
    owned = (mine == iota((16, count), 1) + me * count).astype(jnp.float32)
    loads[1].wait()
    rows = dot(owned, points[:, :count], 1, 1)
    for ch in range(CHUNKS):
        picked[ch] = rows[:, 128 * ch : 128 * ch + 128]
    pl.semaphore_wait(pltpu.get_barrier_semaphore(), greeted)

    my_y = pl.ds(y, 1)
    first = [mail.send("z", s, picked.at[:, pl.ds((z + s) % NZ, 1)], landed.at[s]) for s in far_first(NZ)]
    loads[2].wait()
    pair = [mail.send("c", 1, points.at[pl.ds(0, width), pl.ds(0, count)], points.at[pl.ds(0, width), pl.ds(count, count)])]
    pair.append(mail.send("c", 1, coefs.at[:, pl.ds(0, count)], coefs.at[:, pl.ds(count, count)]))
    loads[3].wait()
    loads[4].wait()

    start = dot(targets[...] - ridge * coefs[:, :count], owned, 1, 1)
    sums[...] = jnp.zeros_like(sums)
    pick, lane = iota((16, 128), 0), iota((16, 128), 1)
    for k in range(nblocks):
        at = (pick // PART == k) & (lane == x * 32 + pick % PART * 8 + y)
        sums[CLASS_ROWS * k : CLASS_ROWS * k + classes, :] = -dot(start, at.astype(jnp.float32))

    arrive(first)
    row = picked[:, pl.ds(z, 1), :]
    for s in range(1, NZ):
        row = row + landed[s]
    my_k, my_i = z // PART, z % PART
    for ch in range(CHUNKS):
        blocks[c, ch, x, my_k, my_i, my_y, :] = row[ch]
    one = blocks.at[c, :, x, my_k, my_i, my_y]
    arrive(mail.spread("z", one, one))

    def along_y(lo, hi):
        some = blocks.at[c, lo:hi, x, :, :, my_y]
        return mail.spread("y", some, some)

    y0 = along_y(0, 2)
    some = blocks.at[c, 2:4, x, :, :, my_y]
    x1 = mail.spread("x", some, some)
    arrive(x1)
    many = blocks.at[c, 2:4, :, :, :, my_y]
    y1 = mail.spread("y", many, many)
    arrive(y0)
    many = blocks.at[c, 0:2, x]
    x0 = mail.spread("x", many, many)

    arrive(pair)
    points_sq = jnp.sum(points[...] * points[...], axis=0, keepdims=True)

    def cross_part(lo):
        half = jnp.concatenate([half_rows(blocks, c, k, lo, lo + 2) for k in range(nblocks)], axis=0)
        squares = jnp.sum(half * half, axis=1, keepdims=True)
        return squares - 2.0 * dot(half, points[128 * lo : 128 * lo + 256, :])

    arrive(x0)
    far[...] = cross_part(0) + points_sq
    arrive(y1)
    other = [mail.send("c", 1, blocks.at[c], blocks.at[c])]
    kern = jnp.exp((far[...] + cross_part(2)) * (-2.0 / width))
    term = dot(coefs[...], kern, 1, 1)
    for k in range(nblocks):
        at = slice(CLASS_ROWS * k, CLASS_ROWS * k + classes)
        sums[at, :] = sums[at, :] + term[:, 128 * k : 128 * k + 128]

    def tall_at(x):
        return pl.ds(pl.multiple_of(x * TALL, TALL), TALL)

    def low_at(y):
        return pl.ds(pl.multiple_of(y * LOW, LOW), LOW)

    sent = [mail.send("x", s, sums.at[tall_at((x + s) % NX)], from_x.at[s]) for s in far_first(NX)]
    role = z % ROLES
    arrive(other)
    own = whole_rows(blocks, role)
    work[:, 256:] = identity(256)
    work[:, :256] = kernel_block(own, own, width) + ridge * identity(256)
    state = factor_groups(factor_start(work, 0), 0, SPLIT)
    arrive(sent)
    value = sums[tall_at(x)]
    for s in range(1, NX):
        value = value + from_x[s]
    sum_x[...] = value
    sent = [mail.send("y", s, sum_x.at[low_at((y + s) % NY)], from_y.at[s]) for s in far_first(NY)]
    factor_end(work, 0, factor_groups(state, SPLIT, 8))
    factor_step(work, 1)
    arrive(sent)
    value = sum_x[low_at(y)]
    for s in range(1, NY):
        value = value + from_y[s]
    sum_y[...] = value
    sent = [mail.send("z", s, sum_y, from_z.at[s]) for s in far_first(NZ)]

    factor_step(work, 2)
    factor_step(work, 3)
    arrive(sent)
    for s in range(1, NZ):
        value = value + from_z[s]
    def piece_of(y):
        return total.at[c, pl.ds(pl.multiple_of(x * TALL + y * LOW, LOW), LOW)]

    mine = piece_of(y)
    mine[...] = value
    down = {s: mail.send("y", s, mine, mine) for s in far_first(NY)}
    across = mail.spread("x", mine, mine)

    gives = {}
    for k in range(ROLES):
        for n, to in enumerate([to for to in range(ROLES) if to != k]):
            gives[k, to] = pltpu.make_async_remote_copy(
                src_ref=solved.at[k],
                dst_ref=solved.at[k],
                send_sem=role_send.at[2 * k + n],
                recv_sem=role_recv.at[k],
                device_id=device(y, x, c, z - role + to),
                device_id_type=MESH,
            )

    def give(k):
        for to in range(ROLES):
            if to != k:
                gives[k, to].start()

    def through(value):
        inverse = work[:, 256:]
        return dot(dot(value, inverse, 1, 1), inverse)

    def own_pick(k):
        pick, lane = iota((16, 256), 0), iota((16, 256), 1)
        at = (pick // PART == k) & (lane == c * 128 + x * 32 + pick % PART * 8 + y)
        return at.astype(jnp.float32)

    def links(j):
        lane, at = iota((256, 256), 1), iota((256, 256), 0)
        line_of = (lane % 8 * NX + lane // 32 % 4) * NC + lane // 128
        order = (at == line_of * PART + lane // 8 % 4).astype(jnp.float32)
        numbers = dot(index_rows[...].astype(jnp.float32), order)
        for n, k in enumerate(range(j + 1, nblocks)):
            column = jnp.sum(jnp.where(at == lane, numbers[k : k + 1, :], 0.0), axis=1, keepdims=True)
            same = (column == numbers[j : j + 1, :]).astype(jnp.float32)
            link[n] = kernel_block(whole_rows(blocks, k), whole_rows(blocks, j), width) + ridge * same

    @pl.when(role == 2)
    def _():
        solved[2] = through(own_pick(2))
        give(2)

    @pl.when(role == 1)
    def _():
        links(1)
        link[0] = through(link[0])
        solved[1] = through(own_pick(1))

    @pl.when(role == 0)
    def _():
        links(0)

    def forward(s):
        arrive([down[s]])
        piece = piece_of((y - s + NY) % NY)
        return mail.spread("x", piece, piece)

    near_first = list(reversed(far_first(NY)))
    for s in near_first[:4]:
        across += forward(s)

    @pl.when(role == 1)
    def _():
        gives[2, 1].wait_recv()
        solved[1] = solved[1] - dot(solved[2], link[0])
        give(1)

    for s in near_first[4:]:
        across += forward(s)

    @pl.when(role == 0)
    def _():
        gives[2, 0].wait_recv()
        value = own_pick(0) - dot(solved[2], link[1])
        gives[1, 0].wait_recv()
        solved[0] = through(value - dot(solved[1], link[0]))
        give(0)

    tall = total.at[c, tall_at(x)]
    sent = [mail.send("c", 1, tall, tall)]

    near = list(reversed(far_first(NX)))
    for n, s in enumerate(near):
        arrive(across[len(near) - 1 - n :: len(near)])
        tall = total.at[c, tall_at((x - s + NX) % NX)]
        sent.append(mail.send("c", 1, tall, tall))
    @pl.when(role == 2)
    def _():
        gives[1, 2].wait_recv()

    @pl.when(role != 0)
    def _():
        gives[0, 1].wait_recv()

    def change_of(cc):
        change = jnp.zeros((classes, 16), jnp.float32)
        for k in range(nblocks):
            rows = total[cc, CLASS_ROWS * k : CLASS_ROWS * k + classes, :]
            at = pl.ds(pl.multiple_of(cc * 128, 128), 128)
            change = change - dot(rows, solved[k, :, at], 1, 1)
        return change

    change = change_of(c)
    arrive(sent)
    change = change + change_of(1 - c)
    out_ref[...] = coefs[:, :count] + dot(change, owned)

    mail.close()

    for k in range(ROLES):

        @pl.when(role == k)
        def _():
            for to in range(ROLES):
                if to != k:
                    gives[k, to].wait_send()


def body(points, targets, coefs, block_index):
    blocks, size = block_index.shape
    count, width = points.shape
    classes = targets.shape[1]
    f32 = jnp.float32
    out = pl.pallas_call(
        whole_body,
        out_shape=jax.ShapeDtypeStruct((classes, count), f32),
        in_specs=[HBM] * 4,
        out_specs=VMEM,
        scratch_shapes=[
            pltpu.SMEM((blocks, size), jnp.int32),
            pltpu.VMEM((128 * CHUNKS, 2 * count), f32),
            pltpu.VMEM((classes, count), f32),
            pltpu.VMEM((classes, 2 * count), f32),
            pltpu.VMEM((blocks, size), jnp.int32),
            pltpu.VMEM((CHUNKS, 16, 128), f32),
            pltpu.VMEM((NZ, CHUNKS, 1, 128), f32),
            pltpu.VMEM((NC, CHUNKS, NX, blocks, PART, NY, 128), f32),
            pltpu.VMEM((blocks * size // 2, 2 * count), f32),
            pltpu.VMEM((PAD, 128), f32),
            pltpu.VMEM((NX, TALL, 128), f32),
            pltpu.VMEM((NY, LOW, 128), f32),
            pltpu.VMEM((NZ, LOW, 128), f32),
            pltpu.VMEM((TALL, 128), f32),
            pltpu.VMEM((LOW, 128), f32),
            pltpu.VMEM((NC, PAD, 128), f32),
            pltpu.VMEM((size, 2 * size), f32),
            pltpu.VMEM((2, size, size), f32),
            pltpu.VMEM((ROLES, 16, size), f32),
            pltpu.SemaphoreType.DMA((5,)),
            pltpu.SemaphoreType.DMA((COPIES,)),
            pltpu.SemaphoreType.DMA((COPIES,)),
            pltpu.SemaphoreType.DMA((2 * ROLES,)),
            pltpu.SemaphoreType.DMA((ROLES,)),
        ],
        compiler_params=pltpu.CompilerParams(vmem_limit_bytes=56307712, collective_id=1, has_side_effects=True),
        name="block_updates",
    )(points.T, targets.T, coefs.T, block_index)
    return out.T


def solution(mesh):
    return jax.shard_map(
        body,
        mesh=mesh,
        in_specs=(
            P(("rows", "grp"), None),
            P(("rows", "grp"), None),
            P(("rows", "grp"), None),
            P(),
        ),
        out_specs=P(("rows", "grp"), None),
        check_vma=False,
    )
```
